256 devices in a mesh: leaf: 8 (over y, core), branch: 32 (over x, z).
Axes of the slice: x: 4, y: 4, z: 8, core: 2. Of those that a mesh axis runs over, the one named last changes fastest.
Arguments:
- queries: bfloat16 [65536, 2560], P(('leaf', 'branch')), parts along dimension 0, may hold values from -4.5 to 4.5
- branch_key_rows: bfloat16 [65536, 512], P(('leaf', 'branch')), parts along dimension 0, may hold values from -4.5 to 4.5
- branch_value_rows: bfloat16 [65536, 512], P(('leaf', 'branch')), parts along dimension 0, may hold values from -4.5 to 4.5
- prefix_keys: bfloat16 [4096, 512], P(('leaf', 'branch')), parts along dimension 0, may hold values from -4.5 to 4.5
- prefix_value_rows: bfloat16 [4096, 512], P(('leaf', 'branch')), parts along dimension 0, may hold values from -4.5 to 4.5
- cotangent: bfloat16 [65536, 2560], P(('leaf', 'branch')), parts along dimension 0, may hold values from -6 to 6
- rewards: int32 [256], P(('leaf', 'branch')), parts along dimension 0, may hold values from 0 to 29, as said below
- lengths: int32 [256], P(('leaf', 'branch')), parts along dimension 0, may hold values from 32 to 256, as said below
- parents: int32 [65536], P(('leaf', 'branch')), parts along dimension 0, may hold values from -1 to 254, as said below
Outputs:
- attended: bfloat16 [65536, 2560], P(('leaf', 'branch')), parts along dimension 0
- grad_queries: bfloat16 [65536, 2560], P(('leaf', 'branch')), parts along dimension 0
- grad_branch_keys: bfloat16 [65536, 512], P(('leaf', 'branch')), parts along dimension 0
- grad_branch_values: bfloat16 [65536, 512], P(('leaf', 'branch')), parts along dimension 0
- grad_prefix_keys: float32 [4096, 512], P(('leaf', 'branch')), parts along dimension 0
- grad_prefix_values: float32 [4096, 512], P(('leaf', 'branch')), parts along dimension 0
The draws below stay inside these ranges and needn't reach their ends.
There are 8 independent parts, one for each index of `leaf`. The reference program is written for one: setup_inputs(seed, part) draws one part's arguments, and reference() takes and returns one part's arrays. A program takes and returns all parts, laid end to end along the dimension named above; each array names one. Nothing has to cross between parts.
Inputs may be any that keep to these rules, and one draw needn't show every extreme that they name: `rewards`: branch b draws its reward from 0 to 9 + 20 * b // 31; the last branch of every tree has the reward 29. `lengths`: some branch of every tree has all 256 slots valid. `parents`: each token's parent is an earlier token of its own branch, given by its position in the branch; the first token of a branch has -1, and the last slot's parent is the slot before it.
All inputs are finite; a program needn't handle non-finite values.
Results may differ from the reference program's by a relative error of at most 0.012.
Values may be sent and summed in bfloat16 or wider, within the bound.
No kernel may reach another device: no remote copies, remote signals or barrier semaphores. Data moves between devices by JAX's collectives and lax.ppermute only.
A program may use at most 128 MiB of HBM per device.

```python
import jax
import jax.numpy as jnp
from jax import lax

QUERY_HEADS = 20
KEY_VALUE_HEADS = 4
HEAD_SIZE = 128
BRANCH_LENGTH = 256
TREE_BRANCHES = 32
TREE_ROWS = 8192
PREFIX_TOKENS = 512


def draw_queries(key, part):
    key = jax.random.fold_in(key, 1)
    sampled_draw = jax.random.normal(key, (TREE_ROWS, QUERY_HEADS * HEAD_SIZE), jnp.float32)
    return jnp.clip(sampled_draw, -4.5, 4.5).astype(jnp.bfloat16)


def draw_prefix_keys(key, part):
    key = jax.random.fold_in(key, 2)
    sampled_draw = jax.random.normal(key, (PREFIX_TOKENS, KEY_VALUE_HEADS * HEAD_SIZE), jnp.float32)
    return jnp.clip(sampled_draw, -4.5, 4.5).astype(jnp.bfloat16)


def draw_rewards(key, part):
    key = jax.random.fold_in(key, 3)
    branch_index = jnp.arange(TREE_BRANCHES, dtype=jnp.int32)
    ceiling = 10 + 20 * branch_index // max(TREE_BRANCHES - 1, 1)
    sampled_draw = jax.random.randint(key, (TREE_BRANCHES,), 0, ceiling)
    return jnp.where(branch_index == TREE_BRANCHES - 1, 29, sampled_draw).astype(jnp.int32)


def draw_lengths(key, part):
    key = jax.random.fold_in(key, 4)
    length_key, chosen_key = jax.random.split(key)
    sampled_draw = jax.random.randint(length_key, (TREE_BRANCHES,), BRANCH_LENGTH // 8, BRANCH_LENGTH + 1)
    chosen = jax.random.randint(chosen_key, (), 0, TREE_BRANCHES)
    return jnp.where(jnp.arange(TREE_BRANCHES) == chosen, BRANCH_LENGTH, sampled_draw).astype(jnp.int32)


def draw_parents(key, part):
    key = jax.random.fold_in(key, 5)
    follow_key, jumped_key = jax.random.split(key)
    places = jnp.arange(TREE_ROWS, dtype=jnp.int32) % BRANCH_LENGTH
    follow = jax.random.randint(follow_key, (TREE_ROWS,), 0, 100) < 85
    jumped = jax.random.randint(jumped_key, (TREE_ROWS,), 0, jnp.maximum(places, 1))
    chosen = jnp.where(follow, places - 1, jumped)
    chosen = jnp.where(places == BRANCH_LENGTH - 1, places - 1, chosen)
    return jnp.where(places == 0, -1, chosen).astype(jnp.int32)


def steps_of(key, shape, cuts, smallest, largest):
    gain = 1.0
    for dim, blocks in cuts:
        draws = jax.random.uniform(jax.random.fold_in(jax.random.fold_in(key, 6), dim), (blocks,), jnp.float32, smallest / len(cuts), largest / len(cuts))
        gain = gain * jnp.repeat(jnp.exp(draws), shape[dim] // blocks).reshape((-1,) + (1,) * (len(shape) - 1 - dim))
    return gain


def noise(stream_key, extent, scale, limit, pieces=(), kind=jnp.bfloat16):
    result = scale * jax.random.normal(stream_key, extent, jnp.float32)
    if pieces:
        result = result * steps_of(stream_key, extent, pieces, -0.22, 0.18)
    return jnp.clip(result, -limit, limit).astype(kind)


def setup_inputs(seed: int = 0, part: int = 0) -> dict:
    splits = jax.random.split(jax.random.key(seed), 10)
    part_keys = jax.random.split(jax.random.fold_in(splits[9], part), 10)
    return {
        "queries": draw_queries(jax.random.fold_in(jax.random.fold_in(splits[9], part), 71), part),
        "branch_key_rows": noise(part_keys[1], (TREE_ROWS, KEY_VALUE_HEADS * HEAD_SIZE), 1.0, 4.5, ((0, 32),)),
        "branch_value_rows": noise(part_keys[2], (TREE_ROWS, KEY_VALUE_HEADS * HEAD_SIZE), 1.0, 4.5, ((0, 32),)),
        "prefix_keys": draw_prefix_keys(jax.random.fold_in(jax.random.fold_in(splits[9], part), 71), part),
        "prefix_value_rows": noise(part_keys[4], (PREFIX_TOKENS, KEY_VALUE_HEADS * HEAD_SIZE), 1.0, 4.5, ((0, 32),)),
        "cotangent": noise(part_keys[5], (TREE_ROWS, QUERY_HEADS * HEAD_SIZE), 1.0, 6.0, ((0, 32),)),
        "rewards": draw_rewards(jax.random.fold_in(jax.random.fold_in(splits[9], part), 71), part),
        "lengths": draw_lengths(jax.random.fold_in(jax.random.fold_in(splits[9], part), 71), part),
        "parents": draw_parents(jax.random.fold_in(jax.random.fold_in(splits[9], part), 71), part),
    }


MASKED = -1.0e30


def ancestry(parents, length_rows):
    places = jnp.arange(length_rows, dtype=jnp.int32)
    one_step = (parents[:, None] == places[None, :]) | (places[:, None] == places[None, :])
    closure = one_step.astype(jnp.float32)
    for squaring in range(max(1, (length_rows - 1).bit_length())):
        closure = jnp.minimum(jnp.dot(closure, closure, precision=lax.Precision.HIGHEST), 1.0)
    return closure > 0.5


def contract(grouped, key_rows):
    blocks = key_rows.reshape(key_rows.shape[0], grouped.shape[1], grouped.shape[3]).astype(jnp.float32)
    return jnp.einsum("tgjd,ngd->gjtn", grouped.astype(jnp.float32), blocks, precision=lax.Precision.HIGHEST)


def mixture(weights, value_rows, grouped):
    blocks = value_rows.reshape(value_rows.shape[0], grouped.shape[1], grouped.shape[3]).astype(jnp.float32)
    return jnp.einsum("gjtn,ngd->gjtd", weights.astype(jnp.float32), blocks, precision=lax.Precision.HIGHEST)


def transposed(weights, grouped):
    product = jnp.einsum("gjtn,tgjd->ngd", weights.astype(jnp.float32), grouped.astype(jnp.float32), precision=lax.Precision.HIGHEST)
    return product.reshape(product.shape[0], -1)


def branch_pass(prefix_keys, prefix_value_rows, advantage, branch_data):
    queries, branch_key_rows, branch_value_rows, cotangent, length, parents = branch_data
    groups = branch_key_rows.shape[1] // HEAD_SIZE
    per_group = queries.shape[1] // (groups * HEAD_SIZE)
    score_scale = HEAD_SIZE ** -0.5
    grouped = queries.reshape(BRANCH_LENGTH, groups, per_group, HEAD_SIZE)
    tree_mask = ancestry(parents, BRANCH_LENGTH)
    score_own = jnp.where(tree_mask[None, None], contract(grouped, branch_key_rows) * score_scale, MASKED)
    score_pre = contract(grouped, prefix_keys) * score_scale
    row_top = jnp.maximum(score_own.max(-1), score_pre.max(-1))
    row_total = jnp.sum(jnp.exp(score_own - row_top[..., None]), -1) + jnp.sum(jnp.exp(score_pre - row_top[..., None]), -1)
    log_total = row_top + jnp.log(row_total)
    prob_own = jnp.exp(score_own - log_total[..., None])
    prob_pre = jnp.exp(score_pre - log_total[..., None])
    weight_own = prob_own.astype(jnp.bfloat16)
    weight_pre = prob_pre.astype(jnp.bfloat16)
    outputs = mixture(weight_own, branch_value_rows, grouped) + mixture(weight_pre, prefix_value_rows, grouped)
    valid_rows = (jnp.arange(BRANCH_LENGTH, dtype=jnp.int32) < length).astype(jnp.float32)
    flat_out = outputs.transpose(2, 0, 1, 3).reshape(BRANCH_LENGTH, QUERY_HEADS * HEAD_SIZE)
    attended = (flat_out * valid_rows[:, None]).astype(jnp.bfloat16)
    weighted = (cotangent.astype(jnp.float32) * advantage * valid_rows[:, None]).astype(jnp.bfloat16)
    weight_grp = weighted.reshape(BRANCH_LENGTH, groups, per_group, HEAD_SIZE)
    delta_rows = jnp.sum(weight_grp.astype(jnp.float32).transpose(1, 2, 0, 3) * outputs, -1)
    dscore_own = (prob_own * (contract(weight_grp, branch_value_rows) - delta_rows[..., None])).astype(jnp.bfloat16)
    dscore_pre = (prob_pre * (contract(weight_grp, prefix_value_rows) - delta_rows[..., None])).astype(jnp.bfloat16)
    grad_rows = score_scale * (mixture(dscore_own, branch_key_rows, grouped) + mixture(dscore_pre, prefix_keys, grouped))
    grad_queries = grad_rows.transpose(2, 0, 1, 3).reshape(BRANCH_LENGTH, QUERY_HEADS * HEAD_SIZE).astype(jnp.bfloat16)
    grad_keys_own = (score_scale * transposed(dscore_own, grouped)).astype(jnp.bfloat16)
    grad_values_own = transposed(weight_own, weight_grp).astype(jnp.bfloat16)
    grad_keys_pre = score_scale * transposed(dscore_pre, grouped)
    grad_values_pre = transposed(weight_pre, weight_grp)
    return attended, grad_queries, grad_keys_own, grad_values_own, grad_keys_pre, grad_values_pre


def reference(queries, branch_key_rows, branch_value_rows, prefix_keys, prefix_value_rows, cotangent, rewards, lengths, parents):
    reward_float = rewards.astype(jnp.float32)
    group_advantages = (reward_float - jnp.sum(reward_float) / TREE_BRANCHES) / 10.0
    stacked_input_rows = (queries.reshape(TREE_BRANCHES, BRANCH_LENGTH, QUERY_HEADS * HEAD_SIZE), branch_key_rows.reshape(TREE_BRANCHES, BRANCH_LENGTH, KEY_VALUE_HEADS * HEAD_SIZE), branch_value_rows.reshape(TREE_BRANCHES, BRANCH_LENGTH, KEY_VALUE_HEADS * HEAD_SIZE), cotangent.reshape(TREE_BRANCHES, BRANCH_LENGTH, QUERY_HEADS * HEAD_SIZE), lengths, parents.reshape(TREE_BRANCHES, BRANCH_LENGTH), group_advantages)

    def visit(running, branch_data):
        results = branch_pass(prefix_keys, prefix_value_rows, branch_data[6], branch_data[:6])
        return (running[0] + results[4], running[1] + results[5]), results[:4]

    blank_holder = jnp.zeros((PREFIX_TOKENS, KEY_VALUE_HEADS * HEAD_SIZE), jnp.float32)
    running_totals, stacked_arrays = lax.scan(visit, (blank_holder, blank_holder), stacked_input_rows)
    return (stacked_arrays[0].reshape(TREE_ROWS, QUERY_HEADS * HEAD_SIZE), stacked_arrays[1].reshape(TREE_ROWS, QUERY_HEADS * HEAD_SIZE), stacked_arrays[2].reshape(TREE_ROWS, KEY_VALUE_HEADS * HEAD_SIZE), stacked_arrays[3].reshape(TREE_ROWS, KEY_VALUE_HEADS * HEAD_SIZE), running_totals[0], running_totals[1])
```

```python
import jax
import jax.numpy as jnp
from jax import lax
from jax.experimental import pallas as pl
from jax.experimental.pallas import tpu as pltpu
from jax.sharding import PartitionSpec as P

HEAD = 128
SCALE = HEAD ** (-0.5)
LOG2E = 1.4426950408889634
MASKED = -1e30
BF = jnp.bfloat16
F32 = jnp.float32
LIMIT = 48 * 1024 * 1024


def nt(a, b):
    return lax.dot_general(a, b, (((1,), (1,)), ((), ())), preferred_element_type=F32)


def nn(a, b):
    return lax.dot_general(a, b, (((1,), (0,)), ((), ())), preferred_element_type=F32)


def tn(a, b):
    return lax.dot_general(a, b, (((0,), (0,)), ((), ())), preferred_element_type=F32)


def head(ref, j):
    return ref[:, j * HEAD : (j + 1) * HEAD]


def ancestry_bias(parents_row, rows):
    child = lax.broadcasted_iota(jnp.int32, (rows, rows), 1)
    place = lax.broadcasted_iota(jnp.int32, (rows, rows), 0)
    step = (parents_row == place) | (child == place)
    closure = jnp.where(step, 1.0, 0.0).astype(BF)
    rounds = max(1, (rows - 1).bit_length())
    for _ in range(rounds - 1):
        closure = jnp.where(nn(closure, closure) > 0.5, 1.0, 0.0).astype(BF)
    counted = lax.dot_general(closure, closure, (((0,), (1,)), ((), ())), preferred_element_type=F32)
    return jnp.where(counted > 0.5, 0.0, MASKED)


def own_forward(per_group, par_ref, q_ref, k_ref, v_ref, p_ref, o_ref, st_ref, bias):
    @pl.when(pl.program_id(0) == 0)
    def _():
        bias[...] = ancestry_bias(par_ref[...], bias.shape[0])

    keys, values = k_ref[...], v_ref[...]
    for j in range(per_group):
        s = nt(head(q_ref, j), keys) * (SCALE * LOG2E) + bias[...]
        m = jnp.max(s, axis=1, keepdims=True)
        p = jnp.exp2(s - m)
        st_ref[0, :, j : j + 1] = m
        st_ref[0, :, 8 + j : 9 + j] = jnp.sum(p, axis=1, keepdims=True)
        pb = p.astype(BF)
        p_ref[j] = pb
        o_ref[:, j * HEAD : (j + 1) * HEAD] = nn(pb, values)


def prefix_forward(
    per_group, branches, len_ref, q_ref, cot_ref, o_ref, st_ref, *rest
):
    chunks = [rest[3 * c : 3 * c + 3] for c in range(4)]
    att_ref, w_ref, wr_ref, qr_ref, p_ref, ds_ref, st2_ref = rest[12:]
    rows = q_ref.shape[0]
    keys = jnp.concatenate([c[0][...] for c in chunks], axis=0)
    values = jnp.concatenate([c[1][...] for c in chunks], axis=0)
    total = sum(jnp.sum(c[2][...].astype(F32), axis=0, keepdims=True) for c in chunks)
    mine = chunks[0][2][0:16, :].astype(F32)[0:1, :]
    advantage = (mine - total / (branches * 16)) / 10.0
    valid = lax.broadcasted_iota(jnp.int32, (rows, HEAD), 0) < len_ref[0]
    factor = jnp.where(valid, advantage, 0.0)
    for j in range(per_group):
        cols = slice(j * HEAD, (j + 1) * HEAD)
        q = q_ref[:, cols]
        w = (cot_ref[:, cols].astype(F32) * factor).astype(BF)
        w_ref[:, cols] = w
        wf = w.astype(F32)
        s = nt(q, keys) * (SCALE * LOG2E)
        m_own = st_ref[0, :, j : j + 1]
        l_own = st_ref[0, :, 8 + j : 9 + j]
        m = jnp.maximum(m_own, jnp.max(s, axis=1, keepdims=True))
        p = jnp.exp2(s - m)
        a_own = jnp.exp2(m_own - m)
        r = 1.0 / (l_own * a_own + jnp.sum(p, axis=1, keepdims=True))
        pb = p.astype(BF)
        p_ref[j] = pb
        out = (nn(pb, values) + o_ref[:, cols] * a_own) * r
        att_ref[:, cols] = jnp.where(valid, out, 0.0).astype(BF)
        delta = jnp.sum(wf * out, axis=1, keepdims=True)
        st2_ref[0, :, j : j + 1] = delta
        st2_ref[0, :, 8 + j : 9 + j] = a_own * r
        st2_ref[0, :, 16 + j : 17 + j] = r
        ds_ref[j] = (p * (nt(w, values) - delta)).astype(BF)
        wr_ref[:, cols] = (wf * r).astype(BF)
        qr_ref[:, cols] = (q.astype(F32) * (r * SCALE)).astype(BF)


def stack(ref, per_group):
    return jnp.concatenate([head(ref, j) for j in range(per_group)], axis=0)


def prefix_grads(per_group, p_ref, ds_ref, qr_ref, wr_ref, g_ref):
    n = p_ref.shape[2]
    rows = p_ref.shape[0] * p_ref.shape[1]
    g_ref[:, :HEAD] = tn(ds_ref[...].reshape(rows, n), stack(qr_ref, per_group)).astype(g_ref.dtype)
    g_ref[:, HEAD:] = tn(p_ref[...].reshape(rows, n), stack(wr_ref, per_group)).astype(g_ref.dtype)


def own_backward(per_group, q_ref, w_ref, k_ref, v_ref, p_ref, ds_ref, st2_ref, c0, c1, c2, c3, dq_ref, dk_ref, dv_ref):
    keys, values = k_ref[...], v_ref[...]
    pre = jnp.concatenate([c[...] for c in (c0, c1, c2, c3)], axis=0)
    dk = jnp.zeros(dk_ref.shape, F32)
    dv = jnp.zeros(dv_ref.shape, F32)
    for j in range(per_group):
        cols = slice(j * HEAD, (j + 1) * HEAD)
        q, w = q_ref[:, cols], w_ref[:, cols]
        delta = st2_ref[0, :, j : j + 1]
        r_own = st2_ref[0, :, 8 + j : 9 + j]
        r = st2_ref[0, :, 16 + j : 17 + j]
        pb = p_ref[j]
        ds = (pb.astype(F32) * (nt(w, values) - delta)).astype(BF)
        dq = (nn(ds_ref[j], pre) * r + nn(ds, keys) * r_own) * SCALE
        dq_ref[:, cols] = dq.astype(BF)
        dk += tn(ds, (q.astype(F32) * (r_own * SCALE)).astype(BF))
        dv += tn(pb, (w.astype(F32) * r_own).astype(BF))
    dk_ref[...] = dk.astype(BF)
    dv_ref[...] = dv.astype(BF)


def exchange(x, bits):
    return lax.ppermute(x, "branch", [(i, i ^ bits) for i in range(lax.axis_size("branch"))])


def on_device(queries, own_keys, own_values, prefix_keys, prefix_values, cotangent, rewards, lengths, parents):
    rows, width = queries.shape
    groups = own_keys.shape[1] // HEAD
    per_group = width // (groups * HEAD)
    gw = per_group * HEAD
    heads = groups * per_group
    shard = prefix_keys.shape[0]
    branches = lax.axis_size("branch")
    npre = shard * branches
    half = groups * HEAD
    params = pltpu.CompilerParams(vmem_limit_bytes=LIMIT, dimension_semantics=("arbitrary",))
    S = jax.ShapeDtypeStruct

    def cols(n, w):
        return pl.BlockSpec((n, w), lambda g: (0, g))

    def per(n, m):
        return pl.BlockSpec((per_group, n, m), lambda g: (g, 0, 0))

    stat = pl.BlockSpec((1, rows, HEAD), lambda g: (g, 0, 0))

    packed = jnp.concatenate(
        [prefix_keys, prefix_values, jnp.broadcast_to(rewards.astype(BF)[:, None], (shard, HEAD))], axis=1
    )
    got = jnp.concatenate([packed, exchange(packed, 6)], axis=0)
    got = jnp.concatenate([got] + [exchange(got, b) for b in (1, 2, 3)], axis=0)
    chunks = [got] + [exchange(got, b * 8) for b in (1, 2, 3)]
    chunk_rows = got.shape[0]

    p_own, o_own, st = pl.pallas_call(
        lambda *refs: own_forward(per_group, *refs),
        grid=(groups,),
        out_shape=(S((heads, rows, rows), BF), S((rows, width), F32), S((groups, rows, HEAD), F32)),
        in_specs=[pl.BlockSpec((1, rows), lambda g: (0, 0)), cols(rows, gw), cols(rows, HEAD), cols(rows, HEAD)],
        out_specs=(per(rows, rows), cols(rows, gw), stat),
        scratch_shapes=[pltpu.VMEM((rows, rows), F32)],
        compiler_params=params,
        cost_estimate=pl.CostEstimate(flops=4 * heads * rows * rows * HEAD * 2, bytes_accessed=8 << 20, transcendentals=heads * rows * rows),
        name="own_forward",
    )(parents.reshape(1, rows), queries, own_keys, own_values)

    def chunk_specs():
        return [
            pl.BlockSpec((chunk_rows, HEAD), lambda g: (0, g)),
            pl.BlockSpec((chunk_rows, HEAD), lambda g: (0, groups + g)),
            pl.BlockSpec((chunk_rows, HEAD), lambda g: (0, 2 * groups)),
        ]

    attended, w, wr, qr, p_pre, ds_pre, st2 = pl.pallas_call(
        lambda *refs: prefix_forward(per_group, branches, *refs),
        grid=(groups,),
        out_shape=(
            S((rows, width), BF),
            S((rows, width), BF),
            S((rows, width), BF),
            S((rows, width), BF),
            S((heads, rows, npre), BF),
            S((heads, rows, npre), BF),
            S((groups, rows, HEAD), F32),
        ),
        in_specs=[pl.BlockSpec(memory_space=pltpu.SMEM), cols(rows, gw), cols(rows, gw), cols(rows, gw), stat]
        + [s for _ in chunks for s in chunk_specs()],
        out_specs=(cols(rows, gw),) * 4 + (per(rows, npre),) * 2 + (stat,),
        compiler_params=params,
        cost_estimate=pl.CostEstimate(flops=6 * heads * rows * npre * HEAD, bytes_accessed=16 << 20, transcendentals=heads * rows * npre),
        name="prefix_forward",
    )(lengths, queries, cotangent, o_own, st, *[c for c in chunks for _ in range(3)])

    def grads_of(c):
        return pl.pallas_call(
            lambda *refs: prefix_grads(per_group, *refs),
            grid=(groups,),
            out_shape=S((chunk_rows, 2 * half), BF),
            in_specs=[pl.BlockSpec((per_group, rows, chunk_rows), lambda g: (g, 0, c))] * 2 + [cols(rows, gw)] * 2,
            out_specs=cols(chunk_rows, 2 * HEAD),
            compiler_params=params,
            cost_estimate=pl.CostEstimate(flops=4 * heads * rows * chunk_rows * HEAD, bytes_accessed=5 << 20, transcendentals=0),
            name=f"prefix_grads_{c}",
        )(p_pre, ds_pre, qr, wr)

    sent = {c: exchange(grads_of(c), c * 8) for c in (2, 1, 3)}

    dq, dk, dv = pl.pallas_call(
        lambda *refs: own_backward(per_group, *refs),
        grid=(groups,),
        out_shape=(S((rows, width), BF), S((rows, half), BF), S((rows, half), BF)),
        in_specs=[cols(rows, gw), cols(rows, gw), cols(rows, HEAD), cols(rows, HEAD), per(rows, rows), per(rows, npre), stat]
        + [pl.BlockSpec((chunk_rows, HEAD), lambda g: (0, g))] * 4,
        out_specs=(cols(rows, gw), cols(rows, HEAD), cols(rows, HEAD)),
        compiler_params=params,
        cost_estimate=pl.CostEstimate(flops=4 * heads * rows * (npre + 3 * rows) * HEAD, bytes_accessed=12 << 20, transcendentals=0),
        name="own_backward",
    )(queries, w, own_keys, own_values, p_own, ds_pre, st2, *chunks)

    def add(parts):
        return sum(p.astype(F32) for p in parts)

    mine = add([grads_of(0)] + [sent[c] for c in (2, 1, 3)]).astype(BF)
    part = mine.reshape(4, 2 * shard, 2 * half)
    mine = add([part[0]] + [exchange(part[b], b) for b in (1, 2, 3)]).astype(BF)
    mine = add([mine[:shard], exchange(mine[shard:], 6)])
    final = mine.reshape(shard, groups, 2, HEAD)
    return (
        attended,
        dq,
        dk,
        dv,
        final[:, :, 0].reshape(shard, half),
        final[:, :, 1].reshape(shard, half),
    )


def solution(mesh):
    split = P(("leaf", "branch"), None)
    line = P(("leaf", "branch"))
    return jax.shard_map(
        on_device,
        mesh=mesh,
        in_specs=(split,) * 6 + (line,) * 3,
        out_specs=(split,) * 6,
        check_vma=False,
    )
```
